128 devices in a mesh: vox: 32 (over z, y, core), ray: 4 (over x).
Axes of the slice: x: 4, y: 4, z: 4, core: 2. Of those that a mesh axis runs over, the one named last changes fastest.
Arguments:
- weights: bfloat16 [1024, 4, 16, 128, 128], P('vox', 'ray'), may hold values from -0.5 to 0.5
- slot_block: int32 [1024, 4, 16], P('vox', 'ray'), may hold values from 0 to 1023
- slot_tile: int32 [1024, 4, 16], P('vox', 'ray'), may hold values from 0 to 63
- slot_count: int32 [1024, 4], P('vox', 'ray'), may hold values from 1 to 16, as said below
- observed: bfloat16 [2048, 4, 128], P('vox', 'ray'), may hold values from -6 to 6
- prior_scale: float32 [32, 128, 1024], P(None, 'vox'), may hold values from 0.2 to 1
Outputs:
- solution: float32 [32, 128, 1024], P(None, 'vox')
- residual: float32 [32, 128, 1024], P(None, 'vox')
The draws below stay inside these ranges and needn't reach their ends.
Inputs may be any that keep to these rules, and one draw needn't show every extreme that they name: `slot_count`: live slots of one bucket, always the first ones; each device has a bucket holding its own largest count, and some bucket of some device holds 16.
All inputs are finite; a program needn't handle non-finite values.
Results may differ from the reference program's by a relative error of at most 0.0059.
Values may be sent and summed in bfloat16 or wider, within the bound.
A program may use at most 64 MiB of HBM per device.

```python
import math
import jax
import jax.numpy as jnp
from jax import lax

NZ = 32
TILE = 128
BLOCK = 128
CXL = 4
NY = 1024
SLOTS = 16
TILES_DEV = 64
ITERS = 2
NX = 128
BLK_DEV = 1024
BUCKETS = 1024
RAY_TILES = 2048
N_VOX = 32
N_RAY = 4


def draw_slot_count(key, part):
    key = jax.random.fold_in(key, 11)
    first, second, third, fourth = jax.random.split(key, 4)
    level = jax.random.randint(first, (N_VOX, N_RAY), max(1, SLOTS // 4), SLOTS + 1)
    chosen = jax.random.randint(second, (), 0, N_VOX * N_RAY)
    places = jnp.arange(N_VOX * N_RAY).reshape(N_VOX, N_RAY)
    level = jnp.where(places == chosen, SLOTS, level)
    spread = jax.random.randint(third, (N_VOX, N_VOX, N_RAY), 0, 1 << 20)
    counts = 1 + spread % level[:, None, :]
    fullest = jax.random.randint(fourth, (N_VOX, 1, N_RAY), 0, N_VOX)
    owners = jnp.arange(N_VOX)[None, :, None]
    counts = jnp.where(owners == fullest, level[:, None, :], counts)
    return counts.reshape(BUCKETS, N_RAY).astype(jnp.int32)


def with_ends(values, own_key, least, high):
    spot = [jax.random.randint(jax.random.fold_in(own_key, axis), (), 0, length) for axis, length in enumerate(values.shape)]
    main_axis = values.shape.index(max(values.shape))
    neighbour = spot[:main_axis] + [(spot[main_axis] + 1) % values.shape[main_axis]] + spot[main_axis + 1:]
    return values.at[tuple(spot)].set(least).at[tuple(neighbour)].set(high)


def levels(key, dims, cuts, smallest, largest):
    level = 1.0
    for position, shards_of in cuts:
        draws = jax.random.uniform(jax.random.fold_in(jax.random.fold_in(key, 6), position), (shards_of,), jnp.float32, smallest / len(cuts), largest / len(cuts))
        level = level * jnp.repeat(jnp.exp(draws), dims[position] // shards_of).reshape((-1,) + (1,) * (len(dims) - 1 - position))
    return level


def scatter_about(rng, extent, scale, bound, cuts=(), kind=jnp.bfloat16):
    values = jax.random.normal(rng, extent, jnp.float32) * scale
    if len(cuts) > 0:
        values = levels(rng, extent, cuts, -0.22, 0.18) * values
    return jnp.clip(values, min=-bound, max=bound).astype(kind)


def setup_inputs(seed: int = 0) -> dict:
    key_list = jax.random.split(jax.random.key(seed), 7)
    return {
        "weights": scatter_about(key_list[0], (BUCKETS, N_RAY, SLOTS, TILE, BLOCK), BLOCK ** -0.5, 0.5, ((0, 32), (1, 4))),
        "slot_block": with_ends(jax.random.randint(key_list[1], (BUCKETS, N_RAY, SLOTS), 0, BLK_DEV), jax.random.fold_in(key_list[1], 1), 0, BLK_DEV - 1).astype(jnp.int32),
        "slot_tile": with_ends(jax.random.randint(key_list[2], (BUCKETS, N_RAY, SLOTS), 0, TILES_DEV), jax.random.fold_in(key_list[2], 1), 0, TILES_DEV - 1).astype(jnp.int32),
        "slot_count": draw_slot_count(jax.random.fold_in(key_list[6], 71), 0),
        "observed": scatter_about(key_list[4], (RAY_TILES, N_RAY, TILE), 1.0, 6.0, ((0, 32), (1, 4))),
        "prior_scale": jnp.clip(jnp.exp(math.log(1.0) - 1.609438 * jax.random.uniform(key_list[5], (NZ, NX, NY), jnp.float32) ** levels(key_list[5], (NZ, NX, NY), ((1, 32),), -0.2, 0.2)), 0.2, 1.0),
    }


def to_blocks(voxel_field):
    return voxel_field.reshape(NZ, N_VOX, CXL, NY).transpose(1, 0, 2, 3).reshape(N_VOX * BLK_DEV, BLOCK)


def from_blocks(block_field):
    return block_field.reshape(N_VOX, NZ, CXL, NY).transpose(1, 0, 2, 3).reshape(NZ, NX, NY)


def laplace(voxel_field):
    padded = jnp.pad(voxel_field, 1)
    beside = padded[2:, 1:-1, 1:-1] + padded[:-2, 1:-1, 1:-1]
    beside = beside + padded[1:-1, 2:, 1:-1] + padded[1:-1, :-2, 1:-1]
    beside = beside + padded[1:-1, 1:-1, 2:] + padded[1:-1, 1:-1, :-2]
    return 6.0 * voxel_field - beside


def reference(weights, slot_block, slot_tile, slot_count, observed, prior_scale):
    highest = lax.Precision.HIGHEST
    grouped_w = weights.reshape(N_VOX, N_VOX, N_RAY, SLOTS, TILE, BLOCK)
    offsets = (jnp.arange(N_VOX, dtype=jnp.int32) * BLK_DEV)[None, :, None, None]
    grouped_b = (slot_block.reshape(N_VOX, N_VOX, N_RAY, SLOTS) + offsets).astype(jnp.int32)
    grouped_t = slot_tile.reshape(N_VOX, N_VOX, N_RAY, SLOTS)
    counts = slot_count.reshape(N_VOX, N_VOX, N_RAY)
    live_mask = (jnp.arange(SLOTS, dtype=jnp.int32)[None, None, None, :] < counts[..., None]).astype(jnp.float32)
    lanes = jnp.arange(N_RAY, dtype=jnp.int32)[None, :, None]
    tile_range = jnp.arange(TILES_DEV, dtype=jnp.int32)

    def forward(direction_low):
        def per_source(pieces):
            weight_src, block_src, tile_src, live_src = pieces
            picked = direction_low[block_src].astype(jnp.float32)
            ray_part = jnp.einsum("urstb,ursb->urst", weight_src.astype(jnp.float32), picked, precision=highest)
            ray_part = ray_part * live_src[..., None]
            onehot = (tile_src[..., None] == tile_range).astype(jnp.float32)
            return jnp.einsum("ursk,urst->krt", onehot, ray_part, precision=highest)

        stacked = lax.map(per_source, (grouped_w, grouped_b, grouped_t, live_mask))
        return stacked.reshape(RAY_TILES, N_RAY, TILE).astype(jnp.bfloat16)

    def transposed(ray_values):
        by_source = ray_values.reshape(N_VOX, TILES_DEV, N_RAY, TILE).transpose(0, 2, 1, 3)

        def per_source(running, pieces):
            weight_src, block_src, tile_src, live_src, rays_src = pieces
            ray_rows = rays_src[lanes, tile_src].astype(jnp.float32)
            voxel_part = jnp.einsum("urstb,urst->ursb", weight_src.astype(jnp.float32), ray_rows, precision=highest)
            voxel_part = voxel_part * live_src[..., None]
            running = running.at[block_src.reshape(-1)].add(voxel_part.reshape(-1, BLOCK))
            return running, None

        start = jnp.zeros((N_VOX * BLK_DEV, BLOCK), jnp.float32)
        return lax.scan(per_source, start, (grouped_w, grouped_b, grouped_t, live_mask, by_source))[0]

    def prior_term(direction):
        scaled = prior_scale * from_blocks(direction)
        return to_blocks(prior_scale * laplace(scaled))

    residual = transposed(observed)
    solution = jnp.zeros_like(residual)
    direction = residual
    norm_now = jnp.sum(residual * residual)
    for iteration in range(ITERS):
        curved = transposed(forward(direction.astype(jnp.bfloat16))) + prior_term(direction)
        step_size = norm_now / jnp.sum(direction * curved)
        solution = solution + step_size * direction
        residual = residual - step_size * curved
        norm_next = jnp.sum(residual * residual)
        direction = residual + (norm_next / norm_now) * direction
        norm_now = norm_next
    return from_blocks(solution), from_blocks(residual)
```

```python
import functools

import jax
import jax.numpy as jnp
from jax import lax
from jax.experimental import pallas as pl
from jax.experimental.pallas import tpu as pltpu
from jax.sharding import PartitionSpec as P

F32 = jnp.float32
BF16 = jnp.bfloat16
MESH = pl.DeviceIdType.MESH
NT = (((1,), (1,)), ((), ()))


def dot(a, b):
    return jnp.dot(a, b, preferred_element_type=F32)


def dot_nt(a, b):
    return lax.dot_general(a, b, NT, preferred_element_type=F32)


def iota(shape, dim):
    return lax.broadcasted_iota(jnp.int32, shape, dim)


def halves(x):
    high = x.astype(BF16)
    return high, (x - high.astype(F32)).astype(BF16)


def block_transpose(a):
    which = lax.rem(iota(a.shape, 1) // 32 - iota(a.shape, 0) // 4 + 4, 4)
    out = a
    for step in range(1, 4):
        moved = pltpu.roll(pltpu.roll(a, 32 * step, 1), 16 - 4 * step, 0)
        out = jnp.where(which == step, moved, out)
    return out


def block_diagonal(rows):
    slots, length = rows.shape
    wide = jnp.concatenate([rows] * slots, axis=1)
    own = iota(wide.shape, 0) == iota(wide.shape, 1) // length
    return jnp.where(own, wide, jnp.zeros_like(wide))


def kernel(
    n_vox, n_ray, dims,
    w_hbm, block_ref, tile_ref, count_ref, observed_ref, prior_ref,
    solution_ref, residual_ref,
    w, onehot, tile_hot, tile_hot_t, ray_rows, ray_part, prior_t,
    id_send, id_recv, prod_send, prod_recv, pick_send, pick_recv,
    scalar_send, scalar_recv, state, halo_x, halo_y, full,
    w_sem, x_send, x_recv, near_send, near_recv, local_sem,
):
    levels, columns, runs, lanes = dims
    n_dev = n_vox * n_ray
    pairs = n_vox // 2
    blocks = levels * columns * runs
    vox = lax.axis_index("vox")
    ray = lax.axis_index("ray")
    me = vox * n_ray + ray

    def pair_at(p):
        return lax.rem(vox // 2 + 1 + p, pairs)

    def w_copy(p):
        at = pl.ds(2 * pair_at(p), 2)
        return pltpu.make_async_copy(w_hbm.at[at], w.at[at], w_sem.at[p])

    def start_w(p, carry):
        w_copy(p).start()
        return carry

    lax.fori_loop(0, pairs, start_w, 0)

    barrier = pltpu.get_barrier_semaphore()

    def target(k):
        t = lax.rem(me + k, n_dev)
        return t, t // n_ray, lax.rem(t, n_ray)

    def greet(k, carry):
        _, tv, tr = target(k)
        pl.semaphore_signal(barrier, 1, device_id=(tv, tr), device_id_type=MESH)
        return carry

    lax.fori_loop(1, n_dev, greet, 0)

    def rows4(index):
        return pl.ds(pl.multiple_of(index * 4, 4), 4)

    def send_tile(src, dst, phase, tv, tr):
        pltpu.make_async_remote_copy(
            src, dst.at[rows4(me)], x_send.at[phase], x_recv.at[phase],
            device_id=(tv, tr), device_id_type=MESH,
        ).start()

    def keep_tile(src, dst):
        copy = pltpu.make_async_copy(src, dst.at[rows4(me)], local_sem)
        copy.start()
        copy.wait()

    def await_tiles(dst, phase, sems, rows):
        part = dst.at[pl.ds(0, (n_dev - 1) * rows)]
        pltpu.make_async_copy(part, part, sems.at[phase]).wait()

    slots = tile_ref.shape[0]
    live = iota((slots, n_vox), 0) < count_ref[...]
    tiles_live = jnp.where(live, tile_ref[...], -1)
    ids = block_ref[...].astype(F32)
    lane = iota((slots, lanes), 1)
    for u in range(n_vox):
        at = pl.ds(u * slots, slots)
        hot = jnp.where(tiles_live[:, u : u + 1] == lane, 1.0, 0.0)
        tile_hot[at] = hot.astype(BF16)
        spread = jnp.broadcast_to(ids[:, u : u + 1], (slots, lanes))
        id_send[pl.ds(u * 4, 4)] = block_transpose(spread)[:4]

    pl.semaphore_wait(barrier, n_dev - 1)

    def send_ids(k, carry):
        _, tv, tr = target(k)
        send_tile(id_send.at[rows4(tv)], id_recv, 0, tv, tr)
        return carry

    lax.fori_loop(1, n_dev, send_ids, 0)
    keep_tile(id_send.at[rows4(vox)], id_recv)

    def transposed(phase, buffer, parts):
        def step(p, carry):
            if phase == 1:
                w_copy(p).wait()
            first = 2 * pair_at(p)
            left = []
            for u in (first, first + 1):
                rows = ray_rows[pl.ds(pl.multiple_of(u * slots, slots), slots)]
                for part in range(parts):
                    left.append(block_diagonal(rows[:, part * lanes : (part + 1) * lanes]))
            right = jnp.concatenate(
                [w[first].reshape(-1, lanes), w[first + 1].reshape(-1, lanes)], axis=1
            )
            made = dot(jnp.concatenate(left, axis=0), right)
            for side, u in enumerate((first, first + 1)):
                columns_of = slice(side * lanes, (side + 1) * lanes)
                base = side * parts * slots
                rows = made[base : base + slots, columns_of]
                for part in range(1, parts):
                    rows = rows + made[base + part * slots : base + (part + 1) * slots, columns_of]
                prod_send[buffer, pl.ds(pl.multiple_of(u * slots, slots), slots)] = (
                    block_transpose(rows)
                )
            for side, u in enumerate((first, first + 1)):
                for k in range(n_ray):
                    tr = lax.rem(ray + k, n_ray)
                    src = prod_send.at[buffer].at[rows4(u * n_ray + tr)]

                    @pl.when(u * n_ray + tr != me)
                    def _():
                        send_tile(src, prod_recv.at[buffer], phase, u, tr)

            return carry

        lax.fori_loop(0, pairs, step, 0)
        keep_tile(prod_send.at[buffer].at[rows4(me)], prod_recv.at[buffer])

    def place(phase, buffer):
        await_tiles(prod_recv.at[buffer], phase, x_recv, 4)
        turned = prod_recv[buffer].T
        rows = turned.shape[1]
        total = None
        for q in range(4):
            high, low = halves(turned[q * 32 : (q + 1) * 32])
            part = dot(
                jnp.concatenate([high, low], axis=0), onehot[q * rows : (q + 1) * rows]
            )
            total = part if total is None else total + part
        return total[:32] + total[32:]

    def gather(phase, buffer, values):
        high, low = halves(values)
        both = jnp.concatenate([high, low], axis=0)
        rows = n_dev * 4
        chunk = rows // 2
        for half in range(2):
            pieces = []
            for q in range(4):
                start = q * rows + half * chunk
                got = dot_nt(both, onehot[start : start + chunk])
                pieces.append(got[:32] + got[32:])
            pick_send[buffer, pl.ds(half * chunk, chunk)] = jnp.concatenate(pieces, axis=0).T

            def send(k, carry):
                t = half * (n_dev // 2) + lax.rem(me + k, n_dev // 2)

                @pl.when(t != me)
                def _():
                    send_tile(
                        pick_send.at[buffer].at[rows4(t)], pick_recv.at[buffer], phase,
                        t // n_ray, lax.rem(t, n_ray),
                    )

                return carry

            lax.fori_loop(0, n_dev // 2, send, 0)
        keep_tile(pick_send.at[buffer].at[rows4(me)], pick_recv.at[buffer])

    def forward(phase, buffer):
        await_tiles(pick_recv.at[buffer], phase, x_recv, 4)

        def step(p, carry):
            left = []
            for side in range(2):
                at = pl.ds(pl.multiple_of((2 * p + side) * slots, slots), slots)
                high, low = halves(block_transpose(pick_recv[buffer, at]))
                left += [block_diagonal(high), block_diagonal(low)]
            right = jnp.concatenate(
                [
                    jnp.concatenate([w[2 * p + side, s] for s in range(slots)], axis=1)
                    for side in range(2)
                ],
                axis=0,
            )
            made = dot_nt(jnp.concatenate(left, axis=0), right)
            for side in range(2):
                at = pl.ds(pl.multiple_of((2 * p + side) * slots, slots), slots)
                columns_of = slice(side * lanes, (side + 1) * lanes)
                for part in range(2):
                    base = (2 * side + part) * slots
                    ray_part[part, at] = made[base : base + slots, columns_of]
            return carry

        lax.fori_loop(0, pairs, step, 0)

        def tiles_of(part):
            values = ray_part[part]
            a, rest = halves(values)
            rest = values - a.astype(F32)
            b = rest.astype(BF16)
            c = (rest - b.astype(F32)).astype(BF16)
            return dot(tile_hot_t[...], a) + dot(tile_hot_t[...], b) + dot(tile_hot_t[...], c)

        return tiles_of(0), tiles_of(1)

    def send_scalars(turn, first, second):
        lane_row = iota((8, lanes), 1)
        scalar_send[turn] = jnp.where(lane_row == 0, first, jnp.where(lane_row == 1, second, 0.0))
        src = scalar_send.at[turn].at[pl.ds(0, 1)]
        dst = scalar_recv.at[turn].at[pl.ds(me, 1)]
        copy = pltpu.make_async_copy(src, dst, local_sem)
        copy.start()
        copy.wait()

        def send(k, carry):
            _, tv, tr = target(k)
            pltpu.make_async_remote_copy(
                src, dst, x_send.at[6 + turn], x_recv.at[6 + turn],
                device_id=(tv, tr), device_id_type=MESH,
            ).start()
            return carry

        lax.fori_loop(1, n_dev, send, 0)

    def await_scalars(turn):
        await_tiles(scalar_recv.at[turn], 6 + turn, x_recv, 1)
        totals = jnp.sum(scalar_recv[turn], axis=0, keepdims=True)
        lane_row = iota((1, lanes), 1)
        first = jnp.sum(jnp.where(lane_row == 0, totals, 0.0), axis=1, keepdims=True)
        second = jnp.sum(jnp.where(lane_row == 1, totals, 0.0), axis=1, keepdims=True)
        return first, second

    def total_of(x):
        return jnp.sum(jnp.sum(x, axis=0, keepdims=True), axis=1, keepdims=True)

    quarter = pl.ds(pl.multiple_of(ray * 32, 32), 32)

    def field_copies(turn):
        src = full.at[turn].at[quarter]
        return [
            pltpu.make_async_remote_copy(
                src, src, near_send.at[turn, k - 1], near_recv.at[turn, k - 1],
                device_id=(vox, lax.rem(ray + k, n_ray)), device_id_type=MESH,
            )
            for k in range(1, n_ray)
        ]

    def halo_copies(turn):
        scaled = state.at[turn]
        right, left = lax.rem(vox + 1, n_vox), lax.rem(vox + n_vox - 1, n_vox)
        after, before = lax.rem(ray + 1, n_ray), lax.rem(ray + n_ray - 1, n_ray)
        plan = [
            (scaled, halo_x.at[turn, 0], (right, ray)),
            (scaled, halo_x.at[turn, 1], (left, ray)),
            (scaled.at[pl.ds(24, 8)], halo_y.at[turn, 0], (vox, after)),
            (scaled.at[pl.ds(0, 8)], halo_y.at[turn, 1], (vox, before)),
        ]
        return [
            pltpu.make_async_remote_copy(
                src, dst, near_send.at[turn, 3 + k], near_recv.at[turn, 3 + k],
                device_id=to, device_id_type=MESH,
            )
            for k, (src, dst, to) in enumerate(plan)
        ]

    def prior(turn):
        for copy in halo_copies(turn):
            copy.wait_recv()
        scaled = state[turn]
        place_of = iota(scaled.shape, 1)
        level = place_of // (columns * runs)
        column = lax.rem(place_of // runs, columns)
        row = iota(scaled.shape, 0)
        step = columns * runs
        zero = jnp.zeros_like(scaled)
        beside = jnp.where(level == 0, zero, pltpu.roll(scaled, step, 1))
        beside += jnp.where(level == levels - 1, zero, pltpu.roll(scaled, blocks - step, 1))
        edge = (columns - 1) * runs
        from_left = jnp.where(vox == 0, zero, pltpu.roll(halo_x[turn, 0], blocks - edge, 1))
        from_right = jnp.where(vox == n_vox - 1, zero, pltpu.roll(halo_x[turn, 1], edge, 1))
        beside += jnp.where(column == 0, from_left, pltpu.roll(scaled, runs, 1))
        beside += jnp.where(column == columns - 1, from_right, pltpu.roll(scaled, blocks - runs, 1))
        run = lax.rem(iota((1, blocks), 1), runs)
        last = halo_y[turn, 0][7:8]
        carried = jnp.where(run == 0, 0.0, pltpu.roll(halo_y[turn, 0], 1, 1)[7:8])
        low_row = jnp.where(ray == 0, carried, last)
        first = halo_y[turn, 1][0:1]
        carried = jnp.where(run == runs - 1, 0.0, pltpu.roll(halo_y[turn, 1], blocks - 1, 1)[0:1])
        high_row = jnp.where(ray == n_ray - 1, carried, first)
        beside += jnp.where(row == 0, low_row, pltpu.roll(scaled, 1, 0))
        beside += jnp.where(row == 31, high_row, pltpu.roll(scaled, 31, 0))
        return prior_t[quarter] * (6.0 * scaled - beside)

    ray_rows[:, :lanes] = dot(tile_hot[:, : observed_ref.shape[0]], observed_ref[...]).astype(BF16)
    transposed(1, 0, 1)
    tile_hot_t[...] = tile_hot[...].astype(F32).T.astype(BF16)
    prior_t[...] = prior_ref[...].T

    await_tiles(id_recv, 0, x_recv, 4)
    rows = n_dev * 4
    number = iota((1, blocks), 1).astype(F32)
    for q in range(4):

        def spread_ids(g, carry):
            at = pl.multiple_of(g * 64, 64)
            own = id_recv[pl.ds(at, 64)][:, q * 32 : q * 32 + 1]
            onehot[pl.ds(q * rows + at, 64)] = jnp.where(own == number, 1.0, 0.0).astype(BF16)
            return carry

        lax.fori_loop(0, rows // 64, spread_ids, 0)

    initial = place(1, 0)
    full[0, quarter] = initial
    gather(2, 0, initial)
    state[0] = prior_t[quarter] * initial
    for copy in halo_copies(0) + field_copies(0):
        copy.start()

    ray_high, ray_low = forward(2, 0)
    tiles = observed_ref.shape[0]
    rounded = ray_high[:tiles].astype(BF16)
    ray_rows[:, :lanes] = dot(tile_hot[:, :tiles], rounded).astype(BF16)
    transposed(3, 1, 1)
    prior_0 = prior(0)
    initial = full[0, quarter]
    curved = place(3, 1) + prior_0
    full[1, quarter] = curved
    gather(4, 1, curved)
    send_scalars(0, total_of(initial * initial), total_of(initial * curved))
    state[1] = prior_t[quarter] * curved
    for copy in halo_copies(1) + field_copies(1):
        copy.start()

    curved_high, curved_low = forward(4, 1)
    norm_0, bend_0 = await_scalars(0)
    step_0 = norm_0 / bend_0
    rays = (ray_high + ray_low) - step_0 * (curved_high + curved_low)
    both = jnp.concatenate(halves(rays[:tiles]), axis=1)
    ray_rows[...] = dot(tile_hot[:, :tiles], both).astype(BF16)
    transposed(5, 2, 2)
    residual = full[0, quarter] - step_0 * full[1, quarter]
    squares = total_of(residual * residual)
    send_scalars(1, squares, squares)
    known = prior_0 - step_0 * prior(1)
    norm_1, _ = await_scalars(1)
    ratio = norm_1 / norm_0
    direction = residual + ratio * full[0, quarter]
    curved = place(5, 2) + known + ratio * full[1, quarter]
    full[2, quarter] = curved
    for copy in field_copies(2):
        copy.start()
    bend = total_of(direction * curved)
    send_scalars(2, bend, bend)

    for turn in range(2):
        for copy in field_copies(turn):
            copy.wait_recv()
    start = full[0]
    residual = start - step_0 * full[1]
    direction = residual + ratio * start
    before = (step_0 * start).T
    residual_t = residual.T
    direction_t = direction.T
    for copy in field_copies(2):
        copy.wait_recv()
    curved_t = full[2].T
    bend_1, _ = await_scalars(2)
    step_1 = norm_1 / bend_1
    solution_ref[...] = before + step_1 * direction_t
    residual_ref[...] = residual_t - step_1 * curved_t

    await_tiles(id_recv, 0, x_send, 4)
    for phase, buffer in ((1, 0), (3, 1), (5, 2)):
        await_tiles(prod_recv.at[buffer], phase, x_send, 4)
    for phase, buffer in ((2, 0), (4, 1)):
        await_tiles(pick_recv.at[buffer], phase, x_send, 4)
    for turn in range(3):
        await_tiles(scalar_recv.at[turn], 6 + turn, x_send, 1)
        for copy in field_copies(turn):
            copy.wait_send()
    for turn in range(2):
        for copy in halo_copies(turn):
            copy.wait_send()


def on_device(weights, slot_block, slot_tile, slot_count, observed, prior_scale):
    n_vox, n_ray = lax.axis_size("vox"), lax.axis_size("ray")
    n_dev = n_vox * n_ray
    levels, columns, across = prior_scale.shape
    slots, lanes = weights.shape[2], weights.shape[4]
    runs = across // lanes
    blocks = levels * columns * runs
    vmem = pl.BlockSpec(memory_space=pltpu.VMEM)
    outs = pl.pallas_call(
        functools.partial(kernel, n_vox, n_ray, (levels, columns, runs, lanes)),
        out_shape=[jax.ShapeDtypeStruct((blocks, lanes), F32)] * 2,
        in_specs=[pl.BlockSpec(memory_space=pl.ANY)] + [vmem] * 5,
        out_specs=[vmem, vmem],
        scratch_shapes=[
            pltpu.VMEM((n_vox, slots, lanes, lanes), BF16),
            pltpu.VMEM((n_dev * slots, blocks), BF16),
            pltpu.VMEM((n_vox * slots, lanes), BF16),
            pltpu.VMEM((lanes, n_vox * slots), BF16),
            pltpu.VMEM((n_vox * slots, 2 * lanes), BF16),
            pltpu.VMEM((2, n_vox * slots, lanes), F32),
            pltpu.VMEM((lanes, blocks), F32),
            pltpu.VMEM((n_vox * 4, lanes), F32),
            pltpu.VMEM((n_dev * 4, lanes), F32),
            pltpu.VMEM((3, n_dev * 4, lanes), F32),
            pltpu.VMEM((3, n_dev * 4, lanes), F32),
            pltpu.VMEM((2, n_dev * 4, lanes), F32),
            pltpu.VMEM((2, n_dev * 4, lanes), F32),
            pltpu.VMEM((3, 8, lanes), F32),
            pltpu.VMEM((3, n_dev, lanes), F32),
            pltpu.VMEM((2, 32, blocks), F32),
            pltpu.VMEM((2, 2, 32, blocks), F32),
            pltpu.VMEM((2, 2, 8, blocks), F32),
            pltpu.VMEM((3, lanes, blocks), F32),
            pltpu.SemaphoreType.DMA((n_vox // 2,)),
            pltpu.SemaphoreType.DMA((9,)),
            pltpu.SemaphoreType.DMA((9,)),
            pltpu.SemaphoreType.DMA((3, 7)),
            pltpu.SemaphoreType.DMA((3, 7)),
            pltpu.SemaphoreType.DMA,
        ],
        compiler_params=pltpu.CompilerParams(
            collective_id=0, has_side_effects=True, vmem_limit_bytes=52 * 2**20
        ),
        name="tomography",
    )(
        weights[:, 0],
        slot_block[:, 0].T,
        slot_tile[:, 0].T,
        slot_count.T,
        observed[:, 0],
        prior_scale.reshape(blocks, lanes),
    )
    return tuple(out.reshape(levels, columns, across) for out in outs)


def solution(mesh):
    in_specs = (
        P("vox", "ray", None, None, None),
        P("vox", "ray", None),
        P("vox", "ray", None),
        P("vox", "ray"),
        P("vox", "ray", None),
        P(None, "vox", None),
    )
    out_specs = (P(None, "vox", None), P(None, "vox", None))
    return jax.shard_map(
        on_device, mesh=mesh, in_specs=in_specs, out_specs=out_specs, check_vma=False
    )
```

```python
import functools

import jax
import jax.numpy as jnp
from jax import lax
from jax.experimental import pallas as pl
from jax.experimental.pallas import tpu as pltpu
from jax.sharding import PartitionSpec as P

F32 = jnp.float32
BF16 = jnp.bfloat16
MESH = pl.DeviceIdType.MESH
NT = (((1,), (1,)), ((), ()))


def dot(a, b):
    return jnp.dot(a, b, preferred_element_type=F32)


def dot_nt(a, b):
    return lax.dot_general(a, b, NT, preferred_element_type=F32)


def iota(shape, dim):
    return lax.broadcasted_iota(jnp.int32, shape, dim)


def halves(x):
    high = x.astype(BF16)
    return high, (x - high.astype(F32)).astype(BF16)


def block_transpose(a):
    which = lax.rem(iota(a.shape, 1) // 32 - iota(a.shape, 0) // 4 + 4, 4)
    out = a
    for step in range(1, 4):
        moved = pltpu.roll(pltpu.roll(a, 32 * step, 1), 16 - 4 * step, 0)
        out = jnp.where(which == step, moved, out)
    return out


def block_diagonal(rows):
    slots, length = rows.shape
    wide = jnp.concatenate([rows] * slots, axis=1)
    own = iota(wide.shape, 0) == iota(wide.shape, 1) // length
    return jnp.where(own, wide, jnp.zeros_like(wide))


def kernel(
    n_vox, n_ray, dims,
    w_hbm, block_hbm, tile_hbm, count_hbm, observed_hbm, prior_hbm,
    solution_ref, residual_ref,
    block_ref, tile_ref, count_ref, observed_ref, prior_ref,
    w, onehot, id_wide, tile_hot, tile_hot_t, ray_rows, ray_part, prior_t,
    id_send, id_recv, prod_send, prod_recv, pick_send, pick_recv,
    scalar_ray, scalar_vox, prior_keep, curved_keep, ray_keep, state, face, halo_x, halo_y, own, shared,
    in_sem, w_sem, pick_sem, x_send, x_recv, near_send, near_recv, local_sem,
):
    levels, columns, runs, lanes = dims
    n_dev = n_vox * n_ray
    pairs = n_vox // 2
    blocks = levels * columns * runs
    vox = lax.axis_index("vox")
    ray = lax.axis_index("ray")
    me = vox * n_ray + ray

    small = [
        pltpu.make_async_copy(src, dst, in_sem.at[k])
        for k, (src, dst) in enumerate((
            (tile_hbm, tile_ref), (count_hbm, count_ref), (block_hbm, block_ref),
            (observed_hbm, observed_ref), (prior_hbm, prior_ref),
        ))
    ]
    for copy in small:
        copy.start()

    side_y = 4
    side_z = pairs // side_y
    my_z, my_y = vox // 2 // side_y, lax.rem(vox // 2, side_y)

    def ring(k):
        return k + (k // 2) * (1 - 2 * lax.rem(k, 2))

    def near_pair(p):
        z = lax.rem(my_z + ring(p // side_y), side_z)
        return z * side_y + lax.rem(my_y + ring(lax.rem(p, side_y)), side_y)

    def far_pair(p):
        return near_pair(pairs - 1 - p)

    def w_copy(p):
        at = pl.ds(2 * far_pair(p), 2)
        return pltpu.make_async_copy(w_hbm.at[at], w.at[at], w_sem.at[p])

    barrier = pltpu.get_barrier_semaphore()
    core = lax.rem(vox, 2)
    rays = [lax.rem(ray + k, n_ray) for k in range(n_ray)]

    def peers(pair):
        return [(2 * pair + c, r) for c in range(2) for r in rays]

    def own_peers():
        return [(vox + 1 - 2 * core, r) for r in rays] + [(vox, r) for r in rays[1:]]

    def for_all(act, group=3):
        def step(g, carry):
            for j in range(group):
                for to in peers(far_pair(group * g + j)):
                    act(to)
            return carry

        lax.fori_loop(0, (pairs - 1) // group, step, 0)
        for to in own_peers():
            act(to)

    def for_vox(act, group=3):
        def step(g, carry):
            for j in range(group):
                pair = far_pair(group * g + j)
                act((2 * pair, ray))
                act((2 * pair + 1, ray))
            return carry

        lax.fori_loop(0, (pairs - 1) // group, step, 0)
        act((vox + 1 - 2 * core, ray))

    def greet(to):
        pl.semaphore_signal(barrier, 1, device_id=to, device_id_type=MESH)

    def start_w(p, carry):
        w_copy(p).start()
        return carry

    lax.fori_loop(0, pairs, start_w, 0)
    for_all(greet)

    def rows4(index):
        return pl.ds(pl.multiple_of(index * 4, 4), 4)

    def send_tile(src, dst, phase, to):
        pltpu.make_async_remote_copy(
            src, dst.at[rows4(me)], x_send.at[phase], x_recv.at[phase],
            device_id=to, device_id_type=MESH,
        ).start()

    def keep_tile(src, dst, phase):
        return pltpu.make_async_copy(src, dst.at[rows4(me)], local_sem.at[phase])

    def await_tiles(dst, phase, sems, rows):
        part = dst.at[pl.ds(0, (n_dev - 1) * rows)]
        pltpu.make_async_copy(part, part, sems.at[phase]).wait()

    for copy in small:
        copy.wait()
    slots = tile_ref.shape[0]
    live = iota((slots, n_vox), 0) < count_ref[...]
    tiles_live = jnp.where(live, tile_ref[...], -1)
    ids = jnp.concatenate(
        [block_ref[...].astype(F32), jnp.zeros((lanes - slots, n_vox), F32)], axis=0
    )
    id_send[...] = ids.T.reshape(n_vox, 1, lanes)
    lane = iota((slots, lanes), 1)
    for u in range(n_vox):
        at = pl.ds(u * slots, slots)
        hot = jnp.where(tiles_live[:, u : u + 1] == lane, 1.0, 0.0)
        tile_hot[at] = hot.astype(BF16)

    def send_id(to):
        pltpu.make_async_remote_copy(
            id_send.at[to[0]], id_recv.at[me], x_send.at[0], x_recv.at[0],
            device_id=to, device_id_type=MESH,
        ).start()

    def await_ids(sems):
        part = id_recv.at[pl.ds(0, n_dev - 1)]
        pltpu.make_async_copy(part, part, sems.at[0]).wait()

    def transposed(phase, buffer, parts, midway=None):
        def send(to):
            src = prod_send.at[buffer].at[rows4(to[0] * n_ray + to[1])]
            send_tile(src, prod_recv.at[buffer], phase, to)

        def product(pair):
            left = []
            for u in (2 * pair, 2 * pair + 1):
                rows = ray_rows[pl.ds(pl.multiple_of(u * slots, slots), slots)]
                for part in range(parts):
                    left.append(block_diagonal(rows[:, part * lanes : (part + 1) * lanes]))
            right = jnp.concatenate(
                [w[2 * pair].reshape(-1, lanes), w[2 * pair + 1].reshape(-1, lanes)], axis=1
            )
            made = dot(jnp.concatenate(left, axis=0), right)
            out = []
            for side in range(2):
                columns_of = slice(side * lanes, (side + 1) * lanes)
                base = side * parts * slots
                rows = made[base : base + slots, columns_of]
                for part in range(1, parts):
                    rows = rows + made[base + part * slots : base + (part + 1) * slots, columns_of]
                out.append(block_transpose(rows))
            return jnp.concatenate(out, axis=0)

        def work(places):
            chosen = [far_pair(p) for p in places]
            if phase == 1:
                for p in places:
                    w_copy(p).wait()
            made = [product(pair) for pair in chosen]
            for pair, tile in zip(chosen, made):
                at = pl.ds(pl.multiple_of(pair * 2 * slots, 2 * slots), 2 * slots)
                prod_send[buffer, at] = tile
            return chosen

        group = 3

        def step(g, carry):
            chosen = work([group * g + j for j in range(group)])
            if phase > 1:
                for pair in chosen:
                    for to in peers(pair):
                        send(to)
            return carry

        groups = (pairs - 1) // group
        cut = groups if midway is None else groups * 3 // 5
        lax.fori_loop(0, cut, step, 0)
        if midway is not None:
            midway()
            lax.fori_loop(cut, groups, step, 0)
        work([pairs - 1])
        keep_tile(prod_send.at[buffer].at[rows4(me)], prod_recv.at[buffer], phase).start()
        if phase == 1:
            pl.semaphore_wait(barrier, n_dev - 1)
            for_all(send_id)
            for_all(send)
            id_recv[me] = id_send[vox]
        else:
            for to in own_peers():
                send(to)

    def place(phase, buffer):
        keep_tile(prod_send.at[buffer].at[rows4(me)], prod_recv.at[buffer], phase).wait()
        await_tiles(prod_recv.at[buffer], phase, x_recv, 4)
        turned = prod_recv[buffer].T
        rows = turned.shape[1]
        total = None
        for q in range(4):
            high, low = halves(turned[q * 32 : (q + 1) * 32])
            part = dot(
                jnp.concatenate([high, low], axis=0), onehot[q * rows : (q + 1) * rows]
            )
            total = part if total is None else total + part
        return total[:32] + total[32:]

    def gather(phase, buffer, values):
        high, low = halves(values)
        both = jnp.concatenate([high, low], axis=0)
        rows = n_dev * 4
        chunk = rows // side_z

        def send(to):
            pltpu.make_async_remote_copy(
                pick_send.at[buffer].at[rows4(to[0] * n_ray + to[1])],
                pick_recv.at[buffer].at[rows4(me)],
                x_send.at[phase], pick_sem.at[buffer, vox // 2],
                device_id=to, device_id_type=MESH,
            ).start()

        for near in (0, 1, 3, 2):
            z = lax.rem(my_z + near, side_z)
            picked = [
                onehot[pl.ds(pl.multiple_of(q * rows + z * chunk, chunk), chunk)] for q in range(4)
            ]
            got = dot_nt(both, jnp.concatenate(picked, axis=0))
            got = got[:32] + got[32:]
            pieces = [got[:, q * chunk : (q + 1) * chunk] for q in range(4)]
            pick_send[buffer, pl.ds(pl.multiple_of(z * chunk, chunk), chunk)] = jnp.concatenate(
                pieces, axis=0
            ).T
            for beside in (0, 1, 3, 2):
                pair = z * side_y + lax.rem(my_y + beside, side_y)
                for to in own_peers() if near == beside == 0 else peers(pair):
                    send(to)
        keep_tile(pick_send.at[buffer].at[rows4(me)], pick_recv.at[buffer], phase).start()

    def forward(phase, buffer, midway):
        def work(places, tiles):
            chosen = [near_pair(p) for p in places]
            for pair in chosen:
                at = pl.ds(pl.multiple_of(pair * 2 * slots, 2 * slots), tiles * 4)
                part = pick_recv.at[buffer].at[at]
                pltpu.make_async_copy(part, part, pick_sem.at[buffer, pair]).wait()
            results = []
            for pair in chosen:
                left = []
                for side in range(2):
                    at = pl.ds(pl.multiple_of((2 * pair + side) * slots, slots), slots)
                    high, low = halves(block_transpose(pick_recv[buffer, at]))
                    left += [block_diagonal(high), block_diagonal(low)]
                right = jnp.concatenate(
                    [
                        jnp.concatenate([w[2 * pair + side, s] for s in range(slots)], axis=1)
                        for side in range(2)
                    ],
                    axis=0,
                )
                results.append(dot_nt(jnp.concatenate(left, axis=0), right))
            for pair, made in zip(chosen, results):
                for side in range(2):
                    at = pl.ds(pl.multiple_of((2 * pair + side) * slots, slots), slots)
                    columns_of = slice(side * lanes, (side + 1) * lanes)
                    for part in range(2):
                        base = (2 * side + part) * slots
                        ray_part[part, at] = made[base : base + slots, columns_of]

        group = 3

        def step(g, carry):
            work([group * g + j + 1 for j in range(group)], 2 * n_ray)
            return carry

        keep_tile(pick_send.at[buffer].at[rows4(me)], pick_recv.at[buffer], phase).wait()
        work([0], 2 * n_ray - 1)
        groups = (pairs - 1) // group
        cut = groups * 2 // 5
        lax.fori_loop(0, cut, step, 0)
        midway()
        lax.fori_loop(cut, groups, step, 0)

        def tiles_of(part):
            values = ray_part[part]
            a, rest = halves(values)
            rest = values - a.astype(F32)
            b = rest.astype(BF16)
            c = (rest - b.astype(F32)).astype(BF16)
            return dot(tile_hot_t[...], a) + dot(tile_hot_t[...], b) + dot(tile_hot_t[...], c)

        return tiles_of(0), tiles_of(1)

    lane_row = iota((1, lanes), 1)

    def sum_along_ray(turn, parts):
        row = jnp.zeros((1, lanes), F32)
        for k, part in enumerate(parts):
            row = jnp.where(lane_row == k, part, row)
        scalar_ray[turn, ray] = row
        src = scalar_ray.at[turn, ray]
        for k in range(1, n_ray):
            pltpu.make_async_remote_copy(
                src, src, x_send.at[6 + turn], x_recv.at[6 + turn],
                device_id=(vox, rays[k]), device_id_type=MESH,
            ).start()

    def await_rows(buffer, sems, at, count):
        part = buffer.at[pl.ds(0, count)]
        pltpu.make_async_copy(part, part, sems.at[at]).wait()

    def sum_along_vox(turn):
        await_rows(scalar_ray.at[turn], x_recv, 6 + turn, n_ray - 1)
        scalar_vox[turn, vox] = jnp.sum(scalar_ray[turn], axis=0)
        src = scalar_vox.at[turn, vox]

        def send(to):
            pltpu.make_async_remote_copy(
                src, src, x_send.at[8 + turn], x_recv.at[8 + turn],
                device_id=to, device_id_type=MESH,
            ).start()

        for_vox(send)

    def totals(turn, count):
        await_rows(scalar_vox.at[turn], x_recv, 8 + turn, n_vox - 1)
        row = jnp.sum(scalar_vox[turn], axis=0)
        return [
            jnp.sum(jnp.where(lane_row == k, row, 0.0), axis=1, keepdims=True)
            for k in range(count)
        ]

    def total_of(x):
        return jnp.sum(jnp.sum(x, axis=0, keepdims=True), axis=1, keepdims=True)

    quarter = pl.ds(pl.multiple_of(ray * 32, 32), 32)

    def field_copies(turn):
        src = shared.at[turn].at[quarter]
        return [
            pltpu.make_async_remote_copy(
                src, src, near_send.at[turn, k - 1], near_recv.at[turn, k - 1],
                device_id=(vox, lax.rem(ray + k, n_ray)), device_id_type=MESH,
            )
            for k in range(1, n_ray)
        ]

    def halo_copies(turn):
        scaled = state.at[turn]
        right, left = lax.rem(vox + 1, n_vox), lax.rem(vox + n_vox - 1, n_vox)
        after, before = lax.rem(ray + 1, n_ray), lax.rem(ray + n_ray - 1, n_ray)
        plan = [
            (face.at[turn, 0], halo_x.at[turn, 0], (right, ray)),
            (face.at[turn, 1], halo_x.at[turn, 1], (left, ray)),
            (scaled.at[pl.ds(24, 8)], halo_y.at[turn, 0], (vox, after)),
            (scaled.at[pl.ds(0, 8)], halo_y.at[turn, 1], (vox, before)),
        ]
        return [
            pltpu.make_async_remote_copy(
                src, dst, near_send.at[turn, 3 + k], near_recv.at[turn, 3 + k],
                device_id=to, device_id_type=MESH,
            )
            for k, (src, dst, to) in enumerate(plan)
        ]

    def column_at(size):
        return lax.rem(iota((32, size), 1) // runs, columns)

    def start_prior(turn, field):
        scaled = prior_t[quarter] * field
        state[turn] = scaled
        for side, column in ((0, columns - 1), (1, 0)):
            for k in range(blocks // lanes // columns):
                packed = jnp.zeros((32, lanes), F32)
                for m in range(columns):
                    at = (columns * k + m) * lanes
                    moved = scaled[:, at : at + lanes]
                    shift = (runs * (m - column)) % lanes
                    if shift:
                        moved = pltpu.roll(moved, shift, 1)
                    packed = jnp.where(column_at(lanes) == m, moved, packed)
                face[turn, side, :, k * lanes : (k + 1) * lanes] = packed
        for copy in halo_copies(turn):
            copy.start()

    def unpacked(turn, side, column):
        out = []
        for k in range(blocks // lanes // columns):
            packed = halo_x[turn, side, :, k * lanes : (k + 1) * lanes]
            for m in range(columns):
                shift = (runs * (column - m)) % lanes
                out.append(pltpu.roll(packed, shift, 1) if shift else packed)
        return jnp.concatenate(out, axis=1)

    def prior(turn):
        for copy in halo_copies(turn):
            copy.wait_recv()
        scaled = state[turn]
        place_of = iota(scaled.shape, 1)
        level = place_of // (columns * runs)
        column = lax.rem(place_of // runs, columns)
        row = iota(scaled.shape, 0)
        step = columns * runs
        zero = jnp.zeros_like(scaled)
        beside = jnp.where(level == 0, zero, pltpu.roll(scaled, step, 1))
        beside += jnp.where(level == levels - 1, zero, pltpu.roll(scaled, blocks - step, 1))
        from_left = jnp.where(vox == 0, zero, unpacked(turn, 0, 0))
        from_right = jnp.where(vox == n_vox - 1, zero, unpacked(turn, 1, columns - 1))
        beside += jnp.where(column == 0, from_left, pltpu.roll(scaled, runs, 1))
        beside += jnp.where(column == columns - 1, from_right, pltpu.roll(scaled, blocks - runs, 1))
        run = lax.rem(iota((1, blocks), 1), runs)
        last = halo_y[turn, 0][7:8]
        carried = jnp.where(run == 0, 0.0, pltpu.roll(halo_y[turn, 0], 1, 1)[7:8])
        low_row = jnp.where(ray == 0, carried, last)
        first = halo_y[turn, 1][0:1]
        carried = jnp.where(run == runs - 1, 0.0, pltpu.roll(halo_y[turn, 1], blocks - 1, 1)[0:1])
        high_row = jnp.where(ray == n_ray - 1, carried, first)
        beside += jnp.where(row == 0, low_row, pltpu.roll(scaled, 1, 0))
        beside += jnp.where(row == 31, high_row, pltpu.roll(scaled, 31, 0))
        return prior_t[quarter] * (6.0 * scaled - beside)

    ray_rows[:, :lanes] = dot(tile_hot[:, : observed_ref.shape[0]], observed_ref[...]).astype(BF16)
    transposed(1, 0, 1)
    tile_hot_t[...] = tile_hot[...].astype(F32).T.astype(BF16)
    prior_t[...] = prior_ref[...].reshape(blocks, lanes).T

    await_ids(x_recv)
    rows = n_dev * 4
    number = iota((1, blocks), 1).astype(F32)
    low_slot, low_lane = lax.rem(iota((rows, lanes), 0), 4), iota((rows, lanes), 1)
    fourfold = jnp.where(iota((rows, n_dev), 0) // 4 == iota((rows, n_dev), 1), 1.0, 0.0)
    fourfold = fourfold.astype(BF16)
    id_high, id_low = halves(id_recv[...].reshape(n_dev, lanes))
    repeated = dot(fourfold, id_high) + dot(fourfold, id_low)
    ones = jnp.full((lanes, lanes), 1.0, BF16)
    for q in range(4):
        high, low = halves(jnp.where(low_lane == 4 * q + low_slot, repeated, 0.0))
        id_wide[q] = dot(high, ones) + dot(low, ones)

    def spread_ids(g, carry):
        at = pl.multiple_of(g * 32, 32)
        for q in range(4):
            own = jnp.concatenate([id_wide[q, pl.ds(at, 32)]] * (blocks // lanes), axis=1)
            onehot[pl.ds(q * rows + at, 32)] = jnp.where(own == number, 1.0, 0.0).astype(BF16)
        return carry

    lax.fori_loop(0, rows // 32, spread_ids, 0)

    initial = place(1, 0)
    own[0] = initial
    gather(2, 0, initial)
    start_prior(0, initial)
    shared[0, quarter] = initial.astype(BF16)

    def prior_0():
        for copy in field_copies(0):
            copy.start()
        prior_keep[0] = prior(0)

    tiles = observed_ref.shape[0]
    ray_high, ray_low = forward(2, 0, prior_0)
    rounded = ray_high[:tiles].astype(BF16)
    rays_0 = ray_high[:tiles] + ray_low[:tiles]
    ray_keep[0] = rays_0
    ray_keep[1] = rounded.astype(F32)
    ray_rows[:, :lanes] = dot(tile_hot[:, :tiles], rounded).astype(BF16)
    initial = own[0]
    bend = total_of(rays_0 * rounded.astype(F32)) + total_of(initial * prior_keep[0])
    sum_along_ray(0, [total_of(initial * initial), bend])
    transposed(3, 1, 1, lambda: sum_along_vox(0))
    norm_0, bend_0 = totals(0, 2)
    step_0 = norm_0 / bend_0
    curved = place(3, 1) + prior_keep[0]
    curved_keep[...] = curved
    residual = own[0] - step_0 * curved
    own[1] = residual
    gather(4, 1, residual)
    start_prior(1, residual)
    shared[1, quarter] = residual.astype(BF16)

    def prior_1():
        for copy in field_copies(1):
            copy.start()
        prior_keep[1] = prior(1)

    ray_high, ray_low = forward(4, 1, prior_1)
    rays_1 = ray_high[:tiles] + ray_low[:tiles]
    both = jnp.concatenate(halves(rays_1), axis=1)
    ray_rows[...] = dot(tile_hot[:, :tiles], both).astype(BF16)
    initial, residual = own[0], own[1]
    square = total_of(rays_1 * rays_1) + total_of(residual * prior_keep[1])
    cross = total_of(rays_1 * (ray_keep[0] + ray_keep[1]))
    cross += total_of(initial * prior_keep[1] + residual * prior_keep[0])
    sum_along_ray(1, [total_of(residual * residual), square, cross])
    transposed(5, 2, 2, lambda: sum_along_vox(1))
    norm_1, square, cross = totals(1, 3)
    ratio = norm_1 / norm_0
    step_1 = norm_1 / (square + ratio * (cross + ratio * bend_0))

    for turn in range(2):
        for copy in field_copies(turn):
            copy.wait_recv()
    start, later = shared[0].astype(F32), shared[1].astype(F32)
    solution_ref[...] = (step_0 * start + step_1 * (later + ratio * start)).T
    curved = place(5, 2) + prior_keep[1] + ratio * curved_keep[...]
    shared[2, quarter] = (own[1] - step_1 * curved).astype(BF16)
    for copy in field_copies(2):
        copy.start()
    for copy in field_copies(2):
        copy.wait_recv()
    residual_ref[...] = shared[2].astype(F32).T

    await_ids(x_send)
    for phase, buffer in ((1, 0), (3, 1), (5, 2)):
        await_tiles(prod_recv.at[buffer], phase, x_send, 4)
    for phase, buffer in ((2, 0), (4, 1)):
        await_tiles(pick_recv.at[buffer], phase, x_send, 4)
    for turn in range(2):
        await_rows(scalar_ray.at[turn], x_send, 6 + turn, n_ray - 1)
        await_rows(scalar_vox.at[turn], x_send, 8 + turn, n_vox - 1)
    for turn in range(3):
        for copy in field_copies(turn):
            copy.wait_send()
    for turn in range(2):
        for copy in halo_copies(turn):
            copy.wait_send()


def on_device(weights, slot_block, slot_tile, slot_count, observed, prior_scale):
    n_vox, n_ray = lax.axis_size("vox"), lax.axis_size("ray")
    n_dev = n_vox * n_ray
    levels, columns, across = prior_scale.shape
    slots, lanes = weights.shape[2], weights.shape[4]
    runs = across // lanes
    blocks = levels * columns * runs
    vmem = pl.BlockSpec(memory_space=pltpu.VMEM)
    outs = pl.pallas_call(
        functools.partial(kernel, n_vox, n_ray, (levels, columns, runs, lanes)),
        out_shape=[jax.ShapeDtypeStruct((blocks, lanes), F32)] * 2,
        in_specs=[pl.BlockSpec(memory_space=pltpu.HBM)] * 6,
        out_specs=[vmem, vmem],
        scratch_shapes=[
            pltpu.VMEM((slots, n_vox), jnp.int32),
            pltpu.VMEM((slots, n_vox), jnp.int32),
            pltpu.VMEM((1, n_vox), jnp.int32),
            pltpu.VMEM(observed[:, 0].shape, BF16),
            pltpu.VMEM(prior_scale.shape, F32),
            pltpu.VMEM((n_vox, slots, lanes, lanes), BF16),
            pltpu.VMEM((n_dev * slots, blocks), BF16),
            pltpu.VMEM((4, n_dev * 4, lanes), F32),
            pltpu.VMEM((n_vox * slots, lanes), BF16),
            pltpu.VMEM((lanes, n_vox * slots), BF16),
            pltpu.VMEM((n_vox * slots, 2 * lanes), BF16),
            pltpu.VMEM((2, n_vox * slots, lanes), F32),
            pltpu.VMEM((lanes, blocks), F32),
            pltpu.VMEM((n_vox, 1, lanes), F32),
            pltpu.VMEM((n_dev, 1, lanes), F32),
            pltpu.VMEM((3, n_dev * 4, lanes), F32),
            pltpu.VMEM((3, n_dev * 4, lanes), F32),
            pltpu.VMEM((2, n_dev * 4, lanes), F32),
            pltpu.VMEM((2, n_dev * 4, lanes), F32),
            pltpu.VMEM((2, n_ray, 1, lanes), F32),
            pltpu.VMEM((2, n_vox, 1, lanes), F32),
            pltpu.VMEM((2, 32, blocks), F32),
            pltpu.VMEM((32, blocks), F32),
            pltpu.VMEM((2, observed.shape[0], lanes), F32),
            pltpu.VMEM((2, 32, blocks), F32),
            pltpu.VMEM((2, 2, 32, blocks // columns), F32),
            pltpu.VMEM((2, 2, 32, blocks // columns), F32),
            pltpu.VMEM((2, 2, 8, blocks), F32),
            pltpu.VMEM((2, 32, blocks), F32),
            pltpu.VMEM((3, lanes, blocks), BF16),
            pltpu.SemaphoreType.DMA((5,)),
            pltpu.SemaphoreType.DMA((n_vox // 2,)),
            pltpu.SemaphoreType.DMA((2, n_vox // 2)),
            pltpu.SemaphoreType.DMA((10,)),
            pltpu.SemaphoreType.DMA((10,)),
            pltpu.SemaphoreType.DMA((3, 7)),
            pltpu.SemaphoreType.DMA((3, 7)),
            pltpu.SemaphoreType.DMA((6,)),
        ],
        compiler_params=pltpu.CompilerParams(
            collective_id=0, has_side_effects=True, vmem_limit_bytes=64 * 2**20
        ),
        name="tomography",
    )(
        weights[:, 0],
        slot_block[:, 0].T,
        slot_tile[:, 0].T,
        slot_count.T,
        observed[:, 0],
        prior_scale,
    )
    return tuple(out.reshape(levels, columns, across) for out in outs)


def solution(mesh):
    in_specs = (
        P("vox", "ray", None, None, None),
        P("vox", "ray", None),
        P("vox", "ray", None),
        P("vox", "ray"),
        P("vox", "ray", None),
        P(None, "vox", None),
    )
    out_specs = (P(None, "vox", None), P(None, "vox", None))
    return jax.shard_map(
        on_device, mesh=mesh, in_specs=in_specs, out_specs=out_specs, check_vma=False
    )
```

```python
import functools

import jax
import jax.numpy as jnp
from jax import lax
from jax.experimental import pallas as pl
from jax.experimental.pallas import tpu as pltpu
from jax.sharding import PartitionSpec as P

F32 = jnp.float32
BF16 = jnp.bfloat16
MESH = pl.DeviceIdType.MESH
NT = (((1,), (1,)), ((), ()))


def dot(a, b):
    return jnp.dot(a, b, preferred_element_type=F32)


def dot_nt(a, b):
    return lax.dot_general(a, b, NT, preferred_element_type=F32)


def iota(shape, dim):
    return lax.broadcasted_iota(jnp.int32, shape, dim)


def halves(x):
    high = x.astype(BF16)
    return high, (x - high.astype(F32)).astype(BF16)


def block_transpose(a):
    which = lax.rem(iota(a.shape, 1) // 32 - iota(a.shape, 0) // 4 + 4, 4)
    out = a
    for step in range(1, 4):
        moved = pltpu.roll(pltpu.roll(a, 32 * step, 1), 16 - 4 * step, 0)
        out = jnp.where(which == step, moved, out)
    return out


def block_diagonal(rows):
    slots, length = rows.shape
    wide = jnp.concatenate([rows] * slots, axis=1)
    own = iota(wide.shape, 0) == iota(wide.shape, 1) // length
    return jnp.where(own, wide, jnp.zeros_like(wide))


def kernel(
    n_vox, n_ray, dims,
    w_hbm, block_hbm, tile_hbm, count_hbm, observed_hbm, prior_hbm,
    solution_ref, residual_ref,
    block_ref, tile_ref, count_ref, observed_ref, prior_ref,
    w, onehot, id_wide, tile_hot, tile_hot_t, ray_rows, ray_part, prior_t,
    id_send, id_recv, prod_send, prod_recv, pick_send, pick_recv,
    scalar_ray, scalar_vox, prior_keep, curved_keep, ray_keep, state, face, halo_x, halo_y, own, shared,
    in_sem, w_sem, pick_sem, x_send, x_recv, near_send, near_recv, local_sem,
):
    levels, columns, runs, lanes = dims
    n_dev = n_vox * n_ray
    pairs = n_vox // 2
    blocks = levels * columns * runs
    vox = lax.axis_index("vox")
    ray = lax.axis_index("ray")
    me = vox * n_ray + ray

    small = [
        pltpu.make_async_copy(src, dst, in_sem.at[k])
        for k, (src, dst) in enumerate((
            (tile_hbm, tile_ref), (count_hbm, count_ref), (block_hbm, block_ref),
            (observed_hbm, observed_ref), (prior_hbm, prior_ref),
        ))
    ]
    for copy in small:
        copy.start()

    side_y = 4
    side_z = pairs // side_y
    my_z, my_y = vox // 2 // side_y, lax.rem(vox // 2, side_y)

    def ring(k):
        return k + (k // 2) * (1 - 2 * lax.rem(k, 2))

    def near_pair(p):
        z = lax.rem(my_z + ring(p // side_y), side_z)
        return z * side_y + lax.rem(my_y + ring(lax.rem(p, side_y)), side_y)

    def far_pair(p):
        return near_pair(pairs - 1 - p)

    def w_copy(p):
        at = pl.ds(2 * far_pair(p), 2)
        return pltpu.make_async_copy(w_hbm.at[at], w.at[at], w_sem.at[p])

    barrier = pltpu.get_barrier_semaphore()
    core = lax.rem(vox, 2)
    rays = [lax.rem(ray + k, n_ray) for k in range(n_ray)]

    def peers(pair):
        return [(2 * pair + c, r) for c in range(2) for r in rays]

    def own_peers():
        return [(vox + 1 - 2 * core, r) for r in rays] + [(vox, r) for r in rays[1:]]

    def for_all(act, group=3):
        def step(g, carry):
            for j in range(group):
                for to in peers(far_pair(group * g + j)):
                    act(to)
            return carry

        lax.fori_loop(0, (pairs - 1) // group, step, 0)
        for to in own_peers():
            act(to)

    def for_vox(act, group=3):
        def step(g, carry):
            for j in range(group):
                pair = far_pair(group * g + j)
                act((2 * pair, ray))
                act((2 * pair + 1, ray))
            return carry

        lax.fori_loop(0, (pairs - 1) // group, step, 0)
        act((vox + 1 - 2 * core, ray))

    def greet(to):
        pl.semaphore_signal(barrier, 1, device_id=to, device_id_type=MESH)

    def start_w(p, carry):
        w_copy(p).start()
        return carry

    lax.fori_loop(0, pairs, start_w, 0)
    for_all(greet)

    def rows4(index):
        return pl.ds(pl.multiple_of(index * 4, 4), 4)

    def send_tile(src, dst, phase, to):
        pltpu.make_async_remote_copy(
            src, dst.at[rows4(me)], x_send.at[phase], x_recv.at[phase],
            device_id=to, device_id_type=MESH,
        ).start()

    def keep_tile(src, dst, phase):
        return pltpu.make_async_copy(src, dst.at[rows4(me)], local_sem.at[phase])

    def await_tiles(dst, phase, sems, rows):
        part = dst.at[pl.ds(0, (n_dev - 1) * rows)]
        pltpu.make_async_copy(part, part, sems.at[phase]).wait()

    for copy in small:
        copy.wait()
    slots = tile_ref.shape[0]
    live = iota((slots, n_vox), 0) < count_ref[...]
    tiles_live = jnp.where(live, tile_ref[...], -1)
    ids = jnp.concatenate(
        [block_ref[...].astype(F32), jnp.zeros((lanes - slots, n_vox), F32)], axis=0
    )
    id_send[...] = ids.T.reshape(n_vox, 1, lanes)
    lane = iota((slots, lanes), 1)
    for u in range(n_vox):
        at = pl.ds(u * slots, slots)
        hot = jnp.where(tiles_live[:, u : u + 1] == lane, 1.0, 0.0)
        tile_hot[at] = hot.astype(BF16)

    def send_id(to):
        pltpu.make_async_remote_copy(
            id_send.at[to[0]], id_recv.at[me], x_send.at[0], x_recv.at[0],
            device_id=to, device_id_type=MESH,
        ).start()

    def await_ids(sems):
        part = id_recv.at[pl.ds(0, n_dev - 1)]
        pltpu.make_async_copy(part, part, sems.at[0]).wait()

    def transposed(phase, buffer, parts, midway=None):
        def send(to):
            src = prod_send.at[buffer].at[rows4(to[0] * n_ray + to[1])]
            send_tile(src, prod_recv.at[buffer], phase, to)

        def product(pair):
            left = []
            for u in (2 * pair, 2 * pair + 1):
                rows = ray_rows[pl.ds(pl.multiple_of(u * slots, slots), slots)]
                for part in range(parts):
                    left.append(block_diagonal(rows[:, part * lanes : (part + 1) * lanes]))
            right = jnp.concatenate(
                [w[2 * pair].reshape(-1, lanes), w[2 * pair + 1].reshape(-1, lanes)], axis=1
            )
            made = dot(jnp.concatenate(left, axis=0), right)
            out = []
            for side in range(2):
                columns_of = slice(side * lanes, (side + 1) * lanes)
                base = side * parts * slots
                rows = made[base : base + slots, columns_of]
                for part in range(1, parts):
                    rows = rows + made[base + part * slots : base + (part + 1) * slots, columns_of]
                out.append(block_transpose(rows))
            return jnp.concatenate(out, axis=0)

        def work(places):
            chosen = [far_pair(p) for p in places]
            if phase == 1:
                for p in places:
                    w_copy(p).wait()
            made = [product(pair) for pair in chosen]
            for pair, tile in zip(chosen, made):
                at = pl.ds(pl.multiple_of(pair * 2 * slots, 2 * slots), 2 * slots)
                prod_send[buffer, at] = tile
            return chosen

        group = 3

        def step(g, carry):
            chosen = work([group * g + j for j in range(group)])
            if phase > 1:
                for pair in chosen:
                    for to in peers(pair):
                        send(to)
            return carry

        groups = (pairs - 1) // group
        cut = groups if midway is None else groups * 3 // 5
        lax.fori_loop(0, cut, step, 0)
        if midway is not None:
            midway()
            lax.fori_loop(cut, groups, step, 0)
        work([pairs - 1])
        keep_tile(prod_send.at[buffer].at[rows4(me)], prod_recv.at[buffer], phase).start()
        if phase == 1:
            pl.semaphore_wait(barrier, n_dev - 1)
            for_all(send_id)
            for_all(send)
            id_recv[me] = id_send[vox]
        else:
            for to in own_peers():
                send(to)

    def place(phase, buffer):
        keep_tile(prod_send.at[buffer].at[rows4(me)], prod_recv.at[buffer], phase).wait()
        await_tiles(prod_recv.at[buffer], phase, x_recv, 4)
        turned = prod_recv[buffer].T
        rows = turned.shape[1]
        total = None
        for q in range(4):
            high, low = halves(turned[q * 32 : (q + 1) * 32])
            part = dot(
                jnp.concatenate([high, low], axis=0), onehot[q * rows : (q + 1) * rows]
            )
            total = part if total is None else total + part
        return total[:32] + total[32:]

    def gather(phase, buffer, values):
        high, low = halves(values)
        both = jnp.concatenate([high, low], axis=0)
        rows = n_dev * 4
        chunk = rows // side_z

        def send(to):
            pltpu.make_async_remote_copy(
                pick_send.at[buffer].at[rows4(to[0] * n_ray + to[1])],
                pick_recv.at[buffer].at[rows4(me)],
                x_send.at[phase], pick_sem.at[buffer, vox // 2],
                device_id=to, device_id_type=MESH,
            ).start()

        for near in (0, 1, 3, 2):
            z = lax.rem(my_z + near, side_z)
            picked = [
                onehot[pl.ds(pl.multiple_of(q * rows + z * chunk, chunk), chunk)] for q in range(4)
            ]
            got = dot_nt(both, jnp.concatenate(picked, axis=0))
            got = got[:32] + got[32:]
            pieces = [got[:, q * chunk : (q + 1) * chunk] for q in range(4)]
            pick_send[buffer, pl.ds(pl.multiple_of(z * chunk, chunk), chunk)] = jnp.concatenate(
                pieces, axis=0
            ).T
            for beside in (0, 1, 3, 2):
                pair = z * side_y + lax.rem(my_y + beside, side_y)
                for to in own_peers() if near == beside == 0 else peers(pair):
                    send(to)
        keep_tile(pick_send.at[buffer].at[rows4(me)], pick_recv.at[buffer], phase).start()

    def forward(phase, buffer, midway):
        def work(places, tiles):
            chosen = [near_pair(p) for p in places]
            for pair in chosen:
                at = pl.ds(pl.multiple_of(pair * 2 * slots, 2 * slots), tiles * 4)
                part = pick_recv.at[buffer].at[at]
                pltpu.make_async_copy(part, part, pick_sem.at[buffer, pair]).wait()
            results = []
            for pair in chosen:
                left = []
                for side in range(2):
                    at = pl.ds(pl.multiple_of((2 * pair + side) * slots, slots), slots)
                    high, low = halves(block_transpose(pick_recv[buffer, at]))
                    left += [block_diagonal(high), block_diagonal(low)]
                right = jnp.concatenate(
                    [
                        jnp.concatenate([w[2 * pair + side, s] for s in range(slots)], axis=1)
                        for side in range(2)
                    ],
                    axis=0,
                )
                results.append(dot_nt(jnp.concatenate(left, axis=0), right))
            for pair, made in zip(chosen, results):
                for side in range(2):
                    at = pl.ds(pl.multiple_of((2 * pair + side) * slots, slots), slots)
                    columns_of = slice(side * lanes, (side + 1) * lanes)
                    for part in range(2):
                        base = (2 * side + part) * slots
                        ray_part[part, at] = made[base : base + slots, columns_of]

        group = 3

        def step(g, carry):
            work([group * g + j + 1 for j in range(group)], 2 * n_ray)
            return carry

        keep_tile(pick_send.at[buffer].at[rows4(me)], pick_recv.at[buffer], phase).wait()
        work([0], 2 * n_ray - 1)
        groups = (pairs - 1) // group
        cut = groups * 2 // 5
        lax.fori_loop(0, cut, step, 0)
        midway()
        lax.fori_loop(cut, groups, step, 0)

        def tiles_of(part):
            values = ray_part[part]
            a, rest = halves(values)
            rest = values - a.astype(F32)
            b = rest.astype(BF16)
            c = (rest - b.astype(F32)).astype(BF16)
            return dot(tile_hot_t[...], a) + dot(tile_hot_t[...], b) + dot(tile_hot_t[...], c)

        return tiles_of(0), tiles_of(1)

    lane_row = iota((1, lanes), 1)

    def sum_along_ray(turn, parts):
        row = jnp.zeros((1, lanes), F32)
        for k, part in enumerate(parts):
            row = jnp.where(lane_row == k, part, row)
        scalar_ray[turn, ray] = row
        src = scalar_ray.at[turn, ray]
        for k in range(1, n_ray):
            pltpu.make_async_remote_copy(
                src, src, x_send.at[6 + turn], x_recv.at[6 + turn],
                device_id=(vox, rays[k]), device_id_type=MESH,
            ).start()

    def await_rows(buffer, sems, at, count):
        part = buffer.at[pl.ds(0, count)]
        pltpu.make_async_copy(part, part, sems.at[at]).wait()

    def sum_along_vox(turn):
        await_rows(scalar_ray.at[turn], x_recv, 6 + turn, n_ray - 1)
        scalar_vox[turn, vox] = jnp.sum(scalar_ray[turn], axis=0)
        src = scalar_vox.at[turn, vox]

        def send(to):
            pltpu.make_async_remote_copy(
                src, src, x_send.at[8 + turn], x_recv.at[8 + turn],
                device_id=to, device_id_type=MESH,
            ).start()

        for_vox(send)

    def totals(turn, count):
        await_rows(scalar_vox.at[turn], x_recv, 8 + turn, n_vox - 1)
        row = jnp.sum(scalar_vox[turn], axis=0)
        return [
            jnp.sum(jnp.where(lane_row == k, row, 0.0), axis=1, keepdims=True)
            for k in range(count)
        ]

    def total_of(x):
        return jnp.sum(jnp.sum(x, axis=0, keepdims=True), axis=1, keepdims=True)

    quarter = pl.ds(pl.multiple_of(ray * 32, 32), 32)

    def field_copies(turn):
        src = shared.at[turn].at[quarter]
        return [
            pltpu.make_async_remote_copy(
                src, src, near_send.at[turn, k - 1], near_recv.at[turn, k - 1],
                device_id=(vox, lax.rem(ray + k, n_ray)), device_id_type=MESH,
            )
            for k in range(1, n_ray)
        ]

    def halo_copies(turn):
        scaled = state.at[turn]
        right, left = lax.rem(vox + 1, n_vox), lax.rem(vox + n_vox - 1, n_vox)
        after, before = lax.rem(ray + 1, n_ray), lax.rem(ray + n_ray - 1, n_ray)
        plan = [
            (face.at[turn, 0], halo_x.at[turn, 0], (right, ray)),
            (face.at[turn, 1], halo_x.at[turn, 1], (left, ray)),
            (scaled.at[pl.ds(24, 8)], halo_y.at[turn, 0], (vox, after)),
            (scaled.at[pl.ds(0, 8)], halo_y.at[turn, 1], (vox, before)),
        ]
        return [
            pltpu.make_async_remote_copy(
                src, dst, near_send.at[turn, 3 + k], near_recv.at[turn, 3 + k],
                device_id=to, device_id_type=MESH,
            )
            for k, (src, dst, to) in enumerate(plan)
        ]

    def column_at(size):
        return lax.rem(iota((32, size), 1) // runs, columns)

    def start_prior(turn, field):
        scaled = prior_t[quarter] * field
        state[turn] = scaled
        for side, column in ((0, columns - 1), (1, 0)):
            for k in range(blocks // lanes // columns):
                packed = jnp.zeros((32, lanes), F32)
                for m in range(columns):
                    at = (columns * k + m) * lanes
                    moved = scaled[:, at : at + lanes]
                    shift = (runs * (m - column)) % lanes
                    if shift:
                        moved = pltpu.roll(moved, shift, 1)
                    packed = jnp.where(column_at(lanes) == m, moved, packed)
                face[turn, side, :, k * lanes : (k + 1) * lanes] = packed
        for copy in halo_copies(turn):
            copy.start()

    def unpacked(turn, side, column):
        out = []
        for k in range(blocks // lanes // columns):
            packed = halo_x[turn, side, :, k * lanes : (k + 1) * lanes]
            for m in range(columns):
                shift = (runs * (column - m)) % lanes
                out.append(pltpu.roll(packed, shift, 1) if shift else packed)
        return jnp.concatenate(out, axis=1)

    def prior(turn):
        for copy in halo_copies(turn):
            copy.wait_recv()
        scaled = state[turn]
        place_of = iota(scaled.shape, 1)
        level = place_of // (columns * runs)
        column = lax.rem(place_of // runs, columns)
        row = iota(scaled.shape, 0)
        step = columns * runs
        zero = jnp.zeros_like(scaled)
        beside = jnp.where(level == 0, zero, pltpu.roll(scaled, step, 1))
        beside += jnp.where(level == levels - 1, zero, pltpu.roll(scaled, blocks - step, 1))
        from_left = jnp.where(vox == 0, zero, unpacked(turn, 0, 0))
        from_right = jnp.where(vox == n_vox - 1, zero, unpacked(turn, 1, columns - 1))
        beside += jnp.where(column == 0, from_left, pltpu.roll(scaled, runs, 1))
        beside += jnp.where(column == columns - 1, from_right, pltpu.roll(scaled, blocks - runs, 1))
        run = lax.rem(iota((1, blocks), 1), runs)
        last = halo_y[turn, 0][7:8]
        carried = jnp.where(run == 0, 0.0, pltpu.roll(halo_y[turn, 0], 1, 1)[7:8])
        low_row = jnp.where(ray == 0, carried, last)
        first = halo_y[turn, 1][0:1]
        carried = jnp.where(run == runs - 1, 0.0, pltpu.roll(halo_y[turn, 1], blocks - 1, 1)[0:1])
        high_row = jnp.where(ray == n_ray - 1, carried, first)
        beside += jnp.where(row == 0, low_row, pltpu.roll(scaled, 1, 0))
        beside += jnp.where(row == 31, high_row, pltpu.roll(scaled, 31, 0))
        return prior_t[quarter] * (6.0 * scaled - beside)

    ray_rows[:, :lanes] = dot(tile_hot[:, : observed_ref.shape[0]], observed_ref[...]).astype(BF16)
    transposed(1, 0, 1)
    tile_hot_t[...] = tile_hot[...].astype(F32).T.astype(BF16)
    prior_t[...] = prior_ref[...].reshape(blocks, lanes).T

    await_ids(x_recv)
    rows = n_dev * 4
    number = iota((1, blocks), 1).astype(F32)
    low_slot, low_lane = lax.rem(iota((rows, lanes), 0), 4), iota((rows, lanes), 1)
    fourfold = jnp.where(iota((rows, n_dev), 0) // 4 == iota((rows, n_dev), 1), 1.0, 0.0)
    fourfold = fourfold.astype(BF16)
    id_high, id_low = halves(id_recv[...].reshape(n_dev, lanes))
    repeated = dot(fourfold, id_high) + dot(fourfold, id_low)
    ones = jnp.full((lanes, lanes), 1.0, BF16)
    for q in range(4):
        high, low = halves(jnp.where(low_lane == 4 * q + low_slot, repeated, 0.0))
        id_wide[q] = dot(high, ones) + dot(low, ones)

    def spread_ids(g, carry):
        at = pl.multiple_of(g * 32, 32)
        for q in range(4):
            own = jnp.concatenate([id_wide[q, pl.ds(at, 32)]] * (blocks // lanes), axis=1)
            onehot[pl.ds(q * rows + at, 32)] = jnp.where(own == number, 1.0, 0.0).astype(BF16)
        return carry

    lax.fori_loop(0, rows // 32, spread_ids, 0)

    initial = place(1, 0)
    own[0] = initial
    gather(2, 0, initial)
    start_prior(0, initial)
    shared[0, quarter] = initial.astype(BF16)

    def prior_0():
        for copy in field_copies(0):
            copy.start()
        prior_keep[0] = prior(0)

    tiles = observed_ref.shape[0]
    ray_high, ray_low = forward(2, 0, prior_0)
    rounded = ray_high[:tiles].astype(BF16)
    rays_0 = ray_high[:tiles] + ray_low[:tiles]
    ray_keep[0] = rays_0
    ray_keep[1] = rounded.astype(F32)
    ray_rows[:, :lanes] = dot(tile_hot[:, :tiles], rounded).astype(BF16)
    initial = own[0]
    bend = total_of(rays_0 * rounded.astype(F32)) + total_of(initial * prior_keep[0])
    sum_along_ray(0, [total_of(initial * initial), bend])
    transposed(3, 1, 1, lambda: sum_along_vox(0))
    norm_0, bend_0 = totals(0, 2)
    step_0 = norm_0 / bend_0
    curved = place(3, 1) + prior_keep[0]
    curved_keep[...] = curved
    residual = own[0] - step_0 * curved
    own[1] = residual
    gather(4, 1, residual)
    start_prior(1, residual)
    shared[1, quarter] = residual.astype(BF16)

    def prior_1():
        for copy in field_copies(1):
            copy.start()
        prior_keep[1] = prior(1)

    ray_high, ray_low = forward(4, 1, prior_1)
    rays_1 = ray_high[:tiles] + ray_low[:tiles]
    both = jnp.concatenate(halves(rays_1), axis=1)
    ray_rows[...] = dot(tile_hot[:, :tiles], both).astype(BF16)
    initial, residual = own[0], own[1]
    square = total_of(rays_1 * rays_1) + total_of(residual * prior_keep[1])
    cross = total_of(rays_1 * (ray_keep[0] + ray_keep[1]))
    cross += total_of(initial * prior_keep[1] + residual * prior_keep[0])
    sum_along_ray(1, [total_of(residual * residual), square, cross])
    transposed(5, 2, 2, lambda: sum_along_vox(1))
    norm_1, square, cross = totals(1, 3)
    ratio = norm_1 / norm_0
    step_1 = norm_1 / (square + ratio * (cross + ratio * bend_0))

    def as_field(x):
        return x.T.reshape(levels, columns, runs * lanes)

    for turn in range(2):
        for copy in field_copies(turn):
            copy.wait_recv()
    start, later = shared[0].astype(F32), shared[1].astype(F32)
    solution_ref[...] = as_field(step_0 * start + step_1 * (later + ratio * start))
    curved = place(5, 2) + prior_keep[1] + ratio * curved_keep[...]
    shared[2, quarter] = (own[1] - step_1 * curved).astype(BF16)
    for copy in field_copies(2):
        copy.start()
    for copy in field_copies(2):
        copy.wait_recv()
    residual_ref[...] = as_field(shared[2].astype(F32))

    await_ids(x_send)
    for phase, buffer in ((1, 0), (3, 1), (5, 2)):
        await_tiles(prod_recv.at[buffer], phase, x_send, 4)
    for phase, buffer in ((2, 0), (4, 1)):
        await_tiles(pick_recv.at[buffer], phase, x_send, 4)
    for turn in range(2):
        await_rows(scalar_ray.at[turn], x_send, 6 + turn, n_ray - 1)
        await_rows(scalar_vox.at[turn], x_send, 8 + turn, n_vox - 1)
    for turn in range(3):
        for copy in field_copies(turn):
            copy.wait_send()
    for turn in range(2):
        for copy in halo_copies(turn):
            copy.wait_send()


def hand_over(solution_in, residual_in, solution_out, residual_out, kept, sem):
    part = solution_in.shape[0] // 2
    incoming, outgoing = [], []
    for n, (src, dst) in enumerate(((solution_in, solution_out), (residual_in, residual_out))):
        for k in range(2):
            at = pl.ds(k * part, part)
            incoming.append(pltpu.make_async_copy(src.at[at], kept.at[n, at], sem.at[0, 2 * n + k]))
            outgoing.append(pltpu.make_async_copy(kept.at[n, at], dst.at[at], sem.at[1, 2 * n + k]))
    for copy in incoming:
        copy.start()
    for arrives, leaves in zip(incoming, outgoing):
        arrives.wait()
        leaves.start()
    for copy in outgoing:
        copy.wait()


def on_device(weights, slot_block, slot_tile, slot_count, observed, prior_scale):
    n_vox, n_ray = lax.axis_size("vox"), lax.axis_size("ray")
    n_dev = n_vox * n_ray
    levels, columns, across = prior_scale.shape
    slots, lanes = weights.shape[2], weights.shape[4]
    runs = across // lanes
    blocks = levels * columns * runs
    vmem = pl.BlockSpec(memory_space=pltpu.VMEM)
    outs = pl.pallas_call(
        functools.partial(kernel, n_vox, n_ray, (levels, columns, runs, lanes)),
        out_shape=[jax.ShapeDtypeStruct(prior_scale.shape, F32)] * 2,
        in_specs=[pl.BlockSpec(memory_space=pltpu.HBM)] * 6,
        out_specs=[vmem, vmem],
        scratch_shapes=[
            pltpu.VMEM((slots, n_vox), jnp.int32),
            pltpu.VMEM((slots, n_vox), jnp.int32),
            pltpu.VMEM((1, n_vox), jnp.int32),
            pltpu.VMEM(observed[:, 0].shape, BF16),
            pltpu.VMEM(prior_scale.shape, F32),
            pltpu.VMEM((n_vox, slots, lanes, lanes), BF16),
            pltpu.VMEM((n_dev * slots, blocks), BF16),
            pltpu.VMEM((4, n_dev * 4, lanes), F32),
            pltpu.VMEM((n_vox * slots, lanes), BF16),
            pltpu.VMEM((lanes, n_vox * slots), BF16),
            pltpu.VMEM((n_vox * slots, 2 * lanes), BF16),
            pltpu.VMEM((2, n_vox * slots, lanes), F32),
            pltpu.VMEM((lanes, blocks), F32),
            pltpu.VMEM((n_vox, 1, lanes), F32),
            pltpu.VMEM((n_dev, 1, lanes), F32),
            pltpu.VMEM((3, n_dev * 4, lanes), F32),
            pltpu.VMEM((3, n_dev * 4, lanes), F32),
            pltpu.VMEM((2, n_dev * 4, lanes), F32),
            pltpu.VMEM((2, n_dev * 4, lanes), F32),
            pltpu.VMEM((2, n_ray, 1, lanes), F32),
            pltpu.VMEM((2, n_vox, 1, lanes), F32),
            pltpu.VMEM((2, 32, blocks), F32),
            pltpu.VMEM((32, blocks), F32),
            pltpu.VMEM((2, observed.shape[0], lanes), F32),
            pltpu.VMEM((2, 32, blocks), F32),
            pltpu.VMEM((2, 2, 32, blocks // columns), F32),
            pltpu.VMEM((2, 2, 32, blocks // columns), F32),
            pltpu.VMEM((2, 2, 8, blocks), F32),
            pltpu.VMEM((2, 32, blocks), F32),
            pltpu.VMEM((3, lanes, blocks), BF16),
            pltpu.SemaphoreType.DMA((5,)),
            pltpu.SemaphoreType.DMA((n_vox // 2,)),
            pltpu.SemaphoreType.DMA((2, n_vox // 2)),
            pltpu.SemaphoreType.DMA((10,)),
            pltpu.SemaphoreType.DMA((10,)),
            pltpu.SemaphoreType.DMA((3, 7)),
            pltpu.SemaphoreType.DMA((3, 7)),
            pltpu.SemaphoreType.DMA((6,)),
        ],
        compiler_params=pltpu.CompilerParams(
            collective_id=0, has_side_effects=True, vmem_limit_bytes=64 * 2**20
        ),
        name="tomography",
    )(
        weights[:, 0],
        slot_block[:, 0].T,
        slot_tile[:, 0].T,
        slot_count.T,
        observed[:, 0],
        prior_scale,
    )
    in_hbm = pl.BlockSpec(memory_space=pltpu.HBM)
    return tuple(
        pl.pallas_call(
            hand_over,
            out_shape=[jax.ShapeDtypeStruct(prior_scale.shape, F32)] * 2,
            in_specs=[in_hbm] * 2,
            out_specs=[in_hbm] * 2,
            scratch_shapes=[
                pltpu.VMEM((2,) + prior_scale.shape, F32),
                pltpu.SemaphoreType.DMA((2, 4)),
            ],
            compiler_params=pltpu.CompilerParams(vmem_limit_bytes=64 * 2**20),
            name="hand_over",
        )(*outs)
    )


def solution(mesh):
    in_specs = (
        P("vox", "ray", None, None, None),
        P("vox", "ray", None),
        P("vox", "ray", None),
        P("vox", "ray"),
        P("vox", "ray", None),
        P(None, "vox", None),
    )
    out_specs = (P(None, "vox", None), P(None, "vox", None))
    return jax.shard_map(
        on_device, mesh=mesh, in_specs=in_specs, out_specs=out_specs, check_vma=False
    )
```
